512 devices in a mesh: space: 32 (over z, x_lo), member: 16 (over x_hi, y, core).
Axes of the slice: x: 4 (x_hi: 2, x_lo: 2; x = x_hi * 2 + x_lo), y: 4, z: 16, core: 2. Of those that a mesh axis runs over, the one named last changes fastest.
Arguments:
- prediction_maps: bfloat16 [16, 72, 64, 1440], P('member', None, 'space'), may hold values from -6 to 6
- truth_analysis: float32 [72, 92160], P(None, ('space', 'member')), may hold values from -6 to 6
- reciprocal_spread: float32 [72], replicated, may hold values from 0.3 to 3
- deconv_inputs: bfloat16 [16, 72, 64, 1440], P('member', None, 'space'), may hold values from -6 to 6
- filter_tensor: bfloat16 [5, 5, 72, 72], replicated, may hold values from -0.125 to 0.125
Outputs:
- grad_hidden: bfloat16 [16, 72, 64, 1440], P('member', None, 'space')
- grad_kernel: float32 [5, 5, 72, 72], replicated
The draws below stay inside these ranges and needn't reach their ends.
All inputs are finite; a program needn't handle non-finite values.
Results may differ from the reference program's by a relative error of at most 0.018.
Values may be sent and summed in bfloat16 or wider, within the bound.
A program may use at most 64 MiB of HBM per device.

```python
import math
import jax
import jax.numpy as jnp
from jax import lax

QUANTITY_TOTAL = 72
MERIDIAN_TOTAL = 1440
KW = 5
ENSEMBLE_SIZE = 16
PARALLEL_TOTAL = 64


def shard_levels(own_key, shape, cuts, smallest, largest):
    def one(position, parts):
        heights = jax.random.uniform(jax.random.fold_in(jax.random.fold_in(own_key, 6), position), (parts,), jnp.float32, smallest / len(cuts), largest / len(cuts))
        return jnp.repeat(jnp.exp(heights), shape[position] // parts).reshape((-1,) + (1,) * (len(shape) - position - 1))

    level = one(*cuts[0])
    for cut in cuts[1:]:
        level = level * one(*cut)
    return level


def normal_values(own_key, extent, width, most, cuts=(), kind=jnp.bfloat16):
    entries = jax.random.normal(own_key, extent, jnp.float32) * width
    if len(cuts) > 0:
        entries = shard_levels(own_key, extent, cuts, -0.22, 0.18) * entries
    return jnp.clip(entries, min=-most, max=most).astype(kind)


def setup_inputs(seed: int = 0) -> dict:
    key_list = jax.random.split(jax.random.key(seed), 6)
    prediction_maps = normal_values(key_list[0], (ENSEMBLE_SIZE, QUANTITY_TOTAL, PARALLEL_TOTAL, MERIDIAN_TOTAL), 1.0, 6.0, ((0, 16), (2, 32)))
    truth_analysis = normal_values(key_list[1], (QUANTITY_TOTAL, PARALLEL_TOTAL * MERIDIAN_TOTAL), 1.0, 6.0, ((1, 512),), jnp.float32)
    reciprocal_spread = jnp.clip(jnp.exp(jax.random.uniform(key_list[2], (QUANTITY_TOTAL,), jnp.float32, math.log(0.3), math.log(3.0))), 0.3, 3.0)
    deconv_inputs = normal_values(key_list[3], (ENSEMBLE_SIZE, QUANTITY_TOTAL, PARALLEL_TOTAL, MERIDIAN_TOTAL), 1.0, 6.0, ((0, 16), (2, 32)))
    filter_tensor = normal_values(key_list[4], (KW, KW, QUANTITY_TOTAL, QUANTITY_TOTAL), (KW * KW * QUANTITY_TOTAL) ** -0.5, 0.125)
    return dict(prediction_maps=prediction_maps, truth_analysis=truth_analysis, reciprocal_spread=reciprocal_spread, deconv_inputs=deconv_inputs, filter_tensor=filter_tensor)


smoothing = 1.0

def area_weights(rows_total):
    index = jnp.arange(rows_total, dtype=jnp.float32)
    latitude = (index + 0.5) * (jnp.pi / rows_total) - jnp.pi / 2
    cosine = jnp.cos(latitude)
    return cosine / jnp.mean(cosine)

def direct_term(own, target, scale):
    offset = scale * (own - target[None])
    radius = jnp.sqrt(lax.optimization_barrier(jnp.sum(offset * offset, axis=1, keepdims=True)) + smoothing)
    return scale * offset / radius

def pair_sums(scaled_own, scaled_other):
    own_sq = lax.optimization_barrier(jnp.sum(scaled_own * scaled_own, axis=1))
    other_sq = lax.optimization_barrier(jnp.sum(scaled_other * scaled_other, axis=1))
    inner = jnp.einsum('mcp,ncp->mnp', scaled_own, scaled_other, precision=lax.Precision.HIGHEST)
    spread_sq = own_sq[:, None, :] + other_sq[None, :, :] - 2.0 * inner + smoothing
    inverse = 1.0 / jnp.sqrt(spread_sq)
    total_weight = lax.optimization_barrier(jnp.sum(inverse, axis=1))
    mixture = jnp.einsum('mnp,ncp->mcp', inverse, scaled_other, precision=lax.Precision.HIGHEST)
    return (total_weight, mixture)

def reference(prediction_maps, truth_analysis, reciprocal_spread, deconv_inputs, filter_tensor):
    predicted_maps = prediction_maps.astype(jnp.float32).reshape(ENSEMBLE_SIZE, QUANTITY_TOTAL, PARALLEL_TOTAL * MERIDIAN_TOTAL)
    target = truth_analysis.reshape(QUANTITY_TOTAL, PARALLEL_TOTAL * MERIDIAN_TOTAL)
    scale = reciprocal_spread[None, :, None]
    direct = direct_term(predicted_maps, target, scale)
    scaled = scale * predicted_maps
    total_weight, mixture = pair_sums(scaled, scaled)
    paired = scale * (scaled * total_weight[:, None, :] - mixture)
    terms = (direct - paired / ENSEMBLE_SIZE).reshape(ENSEMBLE_SIZE, QUANTITY_TOTAL, PARALLEL_TOTAL, MERIDIAN_TOTAL)
    weights = area_weights(PARALLEL_TOTAL)
    grad_out = (terms * weights[None, None, :, None]).astype(jnp.bfloat16)

    def per_member(total, pair):
        member_grad, member_hidden = pair
        padded = jnp.pad(member_grad, ((0, 0), (2, 2), (0, 0)))
        wrapped = jnp.concatenate([padded[:, :, -2:], padded, padded[:, :, :2]], axis=2)
        flat_hidden = member_hidden.reshape(QUANTITY_TOTAL, PARALLEL_TOTAL * MERIDIAN_TOTAL)
        back = jnp.zeros((QUANTITY_TOTAL, PARALLEL_TOTAL * MERIDIAN_TOTAL), jnp.float32)
        pieces = []
        for row_shift in range(KW):
            for col_shift in range(KW):
                shifted = wrapped[:, row_shift:row_shift + PARALLEL_TOTAL, col_shift:col_shift + MERIDIAN_TOTAL].reshape(QUANTITY_TOTAL, PARALLEL_TOTAL * MERIDIAN_TOTAL)
                back = back + jnp.dot(filter_tensor[row_shift, col_shift], shifted, preferred_element_type=jnp.float32)
                pieces.append(jnp.dot(flat_hidden, shifted.T, preferred_element_type=jnp.float32))
        stacked = jnp.stack(pieces).reshape(KW, KW, QUANTITY_TOTAL, QUANTITY_TOTAL)
        return (total + stacked, back.astype(jnp.bfloat16).reshape(QUANTITY_TOTAL, PARALLEL_TOTAL, MERIDIAN_TOTAL))
    kernel_total, grad_hidden = lax.scan(per_member, jnp.zeros((KW, KW, QUANTITY_TOTAL, QUANTITY_TOTAL), jnp.float32), (grad_out, deconv_inputs))
    norm_factor = 1.0 / jnp.sqrt(jnp.float32(ENSEMBLE_SIZE * PARALLEL_TOTAL * MERIDIAN_TOTAL))
    return (grad_hidden, kernel_total * norm_factor)
```

```python
import functools

import jax
import jax.numpy as jnp
import numpy as np
from jax import lax
from jax.experimental import pallas as pl
from jax.experimental.pallas import tpu as pltpu
from jax.sharding import PartitionSpec as P

F32 = jnp.float32
BF16 = jnp.bfloat16
SPACE = 32
MEMBER = 16
CH = 72
CP = 80
LON = 1440
LP = 1536
PX = 180
KW = 5
KC = KW * CP
PK = 112
TILES = 9


def reducer_step(t, m):
    return lax.rem(t + 62 - 16 * lax.rem(m, 2), SPACE)


def is_reducer(t, m):
    u = reducer_step(t, m)
    return jnp.logical_and(lax.rem(u, 3) == 0, u <= 3 * (TILES - 1))


def reducer_of(j, m):
    return lax.rem(3 * j + 2 + 16 * lax.rem(m, 2), SPACE)


def lane_index(rows):
    return lax.broadcasted_iota(jnp.int32, (rows, 128), 1)


def packed(wide):
    lane = lane_index(40)
    rest = wide[:, 128:256]
    low = rest[0:40]
    high = jnp.concatenate([rest[40:72], jnp.zeros((8, 128), F32)], axis=0)
    low = jnp.where(lane < PX - 128, low, 0.0)
    high = jnp.where(lane < PX - 128, high, 0.0)
    tail = jnp.where(lane < 64, low, pltpu.roll(high, 64, 1))
    return jnp.concatenate([wide[:, 0:128], tail], axis=0)


def kernel(
    weight_ref,
    pred_ref,
    truth_ref,
    scale_ref,
    hidden_ref,
    filter_ref,
    back_ref,
    kgrad_ref,
    send1,
    recv1,
    scaled,
    trscr,
    fscr,
    send2,
    recv2,
    ext,
    stack,
    wst,
    gka,
    total,
    out_acc,
    ar1_send,
    ar1_recv,
    ar2_send,
    ar2_recv,
    ar3_send,
    ar3_recv,
    ar4_send,
    ar4_recv,
    s1_sem,
    r1_sem,
    s2_sem,
    r2_sem,
    a1_ssem,
    a1_rsem,
    a2_ssem,
    a2_rsem,
    a3_ssem,
    a3_rsem,
    a4_ssem,
    a4_rsem,
):
    s = lax.axis_index("space")
    m = lax.axis_index("member")
    has_prev = s > 0
    has_next = s < SPACE - 1
    reducing = is_reducer(s, m)

    barrier = pltpu.get_barrier_semaphore()

    def greet(space, member):
        pl.semaphore_signal(barrier, inc=1, device_id={"space": space, "member": member})

    def greet_members(d, _):
        greet(s, lax.rem(m + d, MEMBER))
        return 0

    lax.fori_loop(1, MEMBER, greet_members, 0)

    def greet_bands(d, _):
        n = lax.rem(m + d, MEMBER)

        @pl.when(has_prev)
        def _():
            greet(s - 1, n)

        @pl.when(has_next)
        def _():
            greet(s + 1, n)

        return 0

    lax.fori_loop(0, MEMBER, greet_bands, 0)

    def greet_reducers(d, _):
        t = lax.rem(s + d, SPACE)

        @pl.when(jnp.logical_or(reducing, is_reducer(t, m)))
        def _():
            greet(t, m)

        return 0

    lax.fori_loop(1, SPACE, greet_reducers, 0)
    pl.semaphore_wait(
        barrier,
        MEMBER
        - 1
        + jnp.where(has_prev, MEMBER, 0)
        + jnp.where(has_next, MEMBER, 0)
        + jnp.where(reducing, SPACE - 1, TILES),
    )

    def copy1(src, slot, member):
        return pltpu.make_async_remote_copy(
            src_ref=send1.at[src],
            dst_ref=recv1.at[slot],
            send_sem=s1_sem.at[src],
            recv_sem=r1_sem.at[slot],
            device_id={"space": s, "member": member},
        )

    def fields_out(d, _):
        n = lax.rem(m + d, MEMBER)
        row = n // 8
        start = PX * lax.rem(n, 8)
        off = lax.rem(start, 128)
        base = pl.multiple_of(start - off, 128)
        window = pred_ref[row, :, pl.ds(base, 384)].astype(F32)
        wide = pltpu.roll(window, lax.rem(384 - off, 384), 1)[:, 0:256]
        chunk = packed(wide).astype(BF16)

        @pl.when(d < MEMBER)
        def _():
            send1[n] = chunk
            copy1(n, m, n).start()

        @pl.when(d == MEMBER)
        def _():
            recv1[n] = chunk

        return 0

    lax.fori_loop(1, MEMBER + 1, fields_out, 0)

    eye = lax.broadcasted_iota(jnp.int32, (CH, CH), 0) == lax.broadcasted_iota(jnp.int32, (CH, CH), 1)
    scale_col = jnp.sum(jnp.where(eye, scale_ref[...], 0.0), axis=1, keepdims=True)
    lane40 = lane_index(40)
    scale_wide = jnp.broadcast_to(scale_col, (CH, 128))
    scale_pk = packed(jnp.concatenate([scale_wide, scale_wide], axis=1))
    trscr[...] = jnp.zeros_like(trscr)
    trscr[:, 0:PX] = truth_ref[...]
    truth_pk = packed(trscr[...])

    fscr[...] = jnp.zeros_like(fscr)
    wst[...] = jnp.zeros_like(wst)
    for a in range(KW):
        acc = None
        for b in range(KW):
            fscr[0:CH, 0:CH] = filter_ref[a, b].astype(F32)
            part = jnp.concatenate([fscr[...], jnp.zeros((CP, 384), F32)], axis=1)
            if b:
                part = pltpu.roll(part, CP * b, 1)
            acc = part if acc is None else acc + part
        acc = acc.astype(BF16)
        wst[a, 0:CP, :] = acc
        wst[a + 1, CP : 2 * CP, :] = acc
    gka[...] = jnp.zeros_like(gka)
    out_acc[...] = jnp.zeros_like(out_acc)

    def fields_in(d, _):
        n = lax.rem(m + MEMBER - d, MEMBER)

        @pl.when(d < MEMBER)
        def _():
            copy1(n, n, n).wait_recv()

        scaled[n] = scale_pk * recv1[n].astype(F32)
        return 0

    lax.fori_loop(1, MEMBER + 1, fields_in, 0)

    weight = weight_ref[2 * s + m // 8]

    def copy2(kind, src, slot, space, member):
        return pltpu.make_async_remote_copy(
            src_ref=send2.at[src],
            dst_ref=recv2.at[kind, slot],
            send_sem=s2_sem.at[kind, src],
            recv_sem=r2_sem.at[kind, slot],
            device_id={"space": space, "member": member},
        )

    def column_sums(square):
        main = jnp.sum(square[0:CH], axis=0, keepdims=True)
        tail = jnp.sum(square[CH:PK], axis=0, keepdims=True)
        return main, tail + pltpu.roll(tail, 64, 1)

    def spread_out(main, tail):
        return jnp.concatenate(
            [jnp.broadcast_to(main, (CH, 128)), jnp.broadcast_to(tail, (PK - CH, 128))], axis=0
        )

    def gradient(d, _):
        n = lax.rem(m + d, MEMBER)
        y = scaled[n]
        offset = scale_pk * (recv1[n].astype(F32) - truth_pk)
        main, tail = column_sums(offset * offset)
        direct = scale_pk * offset * spread_out(lax.rsqrt(main + 1.0), lax.rsqrt(tail + 1.0))

        def pair(k, mix):
            diff = scaled[k] - y
            main, tail = column_sums(diff * diff)
            return mix + diff * spread_out(lax.rsqrt(main + 1.0), lax.rsqrt(tail + 1.0))

        mix = lax.fori_loop(0, MEMBER, pair, jnp.zeros((PK, 128), F32), unroll=4)
        grad = (weight * (direct + scale_pk * mix * (1.0 / MEMBER))).astype(BF16)
        send2[n] = grad

        @pl.when(d < MEMBER)
        def _():
            copy2(1, n, m, s, n).start()

        @pl.when(d == MEMBER)
        def _():
            recv2[1, n] = grad

        return 0

    lax.fori_loop(1, MEMBER + 1, gradient, 0)

    def halo_prev(d, _):
        n = lax.rem(m + d, MEMBER)

        @pl.when(has_prev)
        def _():
            copy2(2, n, m, s - 1, n).start()

        return 0

    def halo_next(d, _):
        n = lax.rem(m + d, MEMBER)

        @pl.when(has_next)
        def _():
            copy2(0, n, m, s + 1, n).start()

        return 0

    lax.fori_loop(0, MEMBER, halo_prev, 0)
    lax.fori_loop(0, MEMBER, halo_next, 0)

    def wait_block(kind):
        def one(d, _):
            n = lax.rem(m + MEMBER - d, MEMBER)

            @pl.when(jnp.logical_or(kind != 1, d > 0))
            def _():
                copy2(kind, n, n, s, n).wait_recv()

            return 0

        lax.fori_loop(0, MEMBER, one, 0)

    def rows_ready(kind, half):
        q = 2 * kind + half
        ext[...] = jnp.zeros_like(ext)
        lane = lane40
        for k in range(8):
            chunk = recv2[kind, 8 * half + k].astype(F32)
            tail = chunk[CH:PK]
            low = jnp.where(lane < PX - 128, tail, 0.0)
            high = jnp.where(lane < PX - 128, pltpu.roll(tail, 64, 1), 0.0)
            rest = jnp.concatenate([low, high[0:32]], axis=0)
            wide = jnp.concatenate([chunk[0:CH], rest, jnp.zeros((CH, 128), F32)], axis=1)
            start = PX * k + 2
            base, off = start // 128 * 128, start % 128
            ext[0:CH, base : base + 384] += pltpu.roll(wide, off, 1)
        first = ext[:, 0:128]
        last = ext[:, LP - 128 : LP]
        lane80 = lane_index(CP)
        ext[:, 0:128] = jnp.where(lane80 < 2, pltpu.roll(last, 96, 1), first)
        ext[:, LP - 128 : LP] = jnp.where(
            jnp.logical_and(lane80 >= 34, lane80 < 36), pltpu.roll(first, 32, 1), last
        )
        for g in range(CP // 16):
            rows = ext[16 * g : 16 * g + 16, :]
            for b in range(KW):
                moved = rows if b == 0 else pltpu.roll(rows, LP - b, 1)
                at = pl.multiple_of((KW * q + b) * CP + 16 * g, 16)
                stack[pl.ds(at, 16), :] = moved.astype(BF16)

    def stacked(q):
        return stack[pl.ds(pl.multiple_of(q * KC, 16), KC), :]

    def kernel_terms(q):
        product = lax.dot_general(
            hidden_ref[...], stacked(q), (((1,), (1,)), ((), ())), preferred_element_type=F32
        )
        up = jnp.minimum(q, KW - 1)
        down = jnp.maximum(q - 1, 0)

        @pl.when(q < KW)
        def _():
            gka[up, :, 0:KC] += product[0:CP]

        @pl.when(q > 0)
        def _():
            gka[down, :, 0:KC] += product[CP : 2 * CP]

    def hidden_terms(q):
        out_acc[...] += jnp.dot(wst[q, :, 0:KC], stacked(q), preferred_element_type=F32)

    def present(kind):
        return jnp.logical_and(
            jnp.logical_or(kind != 0, has_prev), jnp.logical_or(kind != 2, has_next)
        )

    def block(i, _):
        kind = lax.rem(i + 1, 3)

        @pl.when(present(kind))
        def _():
            wait_block(kind)

            def half_step(half, _):
                rows_ready(kind, half)
                kernel_terms(2 * kind + half)

                @pl.when(i < 2)
                def _():
                    hidden_terms(2 * kind + half)

                return 0

            lax.fori_loop(0, 2, half_step, 0)

        return 0

    lax.fori_loop(0, 3, block, 0)

    total[...] = jnp.zeros_like(total)
    for a in range(KW):
        base, off = KC * a // 128 * 128, KC * a % 128
        part = gka[a]
        total[:, base : base + 512] += pltpu.roll(part, off, 1) if off else part

    def copy_a1(src, slot, member):
        return pltpu.make_async_remote_copy(
            src_ref=ar1_send.at[src],
            dst_ref=ar1_recv.at[slot],
            send_sem=a1_ssem.at[src],
            recv_sem=a1_rsem.at[slot],
            device_id={"space": s, "member": member},
        )

    def shares_out(d, _):
        n = lax.rem(m + d, MEMBER)
        ar1_send[n] = total[:, pl.ds(pl.multiple_of(128 * n, 128), 128)].astype(BF16)
        copy_a1(n, m, n).start()
        return 0

    lax.fori_loop(1, MEMBER, shares_out, 0)

    @pl.when(has_prev)
    def _():
        hidden_terms(0)
        hidden_terms(1)

    back_ref[0] = out_acc[0:CH, 0:LON].astype(BF16)
    back_ref[1] = out_acc[CP : CP + CH, 0:LON].astype(BF16)

    def shares_in(d, acc):
        n = lax.rem(m + MEMBER - d, MEMBER)
        copy_a1(n, n, n).wait_recv()
        return acc + ar1_recv[n].astype(F32)

    own = total[:, pl.ds(pl.multiple_of(128 * m, 128), 128)]
    share = lax.fori_loop(1, MEMBER, shares_in, own)

    for j in range(TILES):
        ar2_send[j] = share[8 * j : 8 * j + 8]

    def copy_a2(j, slot, space):
        return pltpu.make_async_remote_copy(
            src_ref=ar2_send.at[j],
            dst_ref=ar2_recv.at[slot],
            send_sem=a2_ssem.at[j],
            recv_sem=a2_rsem.at[slot],
            device_id={"space": space, "member": m},
        )

    def tiles_out(j, _):
        t = reducer_of(j, m)

        @pl.when(t != s)
        def _():
            copy_a2(j, s, t).start()

        return 0

    lax.fori_loop(0, TILES, tiles_out, 0)
    mine = jnp.minimum(reducer_step(s, m) // 3, TILES - 1)
    norm = float(1.0 / np.sqrt(np.float32(MEMBER * 2 * SPACE * LON)))

    def copy_a3(j, t, space):
        return pltpu.make_async_remote_copy(
            src_ref=ar3_send,
            dst_ref=ar3_recv.at[j],
            send_sem=a3_ssem.at[t],
            recv_sem=a3_rsem.at[j],
            device_id={"space": space, "member": m},
        )

    @pl.when(reducing)
    def _():
        def tiles_in(d, acc):
            t = lax.rem(s + SPACE - d, SPACE)
            copy_a2(0, t, t).wait_recv()
            return acc + ar2_recv[t]

        tile = lax.fori_loop(1, SPACE, tiles_in, ar2_send[mine]) * norm
        ar3_send[...] = tile
        ar3_recv[mine] = tile

        def tile_to(d, _):
            t = lax.rem(s + d, SPACE)
            copy_a3(mine, t, t).start()
            return 0

        lax.fori_loop(1, SPACE, tile_to, 0)

    def tiles_back(j, _):
        t = reducer_of(j, m)

        @pl.when(t != s)
        def _():
            copy_a3(j, 0, t).wait_recv()

        return 0

    lax.fori_loop(0, TILES, tiles_back, 0)

    final = jnp.concatenate([ar3_recv[j] for j in range(TILES)] + [jnp.zeros((8, 128), F32)], axis=0)
    ar4_send[...] = final.astype(BF16)
    total[:, pl.ds(pl.multiple_of(128 * m, 128), 128)] = final

    def copy_a4(n, slot, member):
        return pltpu.make_async_remote_copy(
            src_ref=ar4_send,
            dst_ref=ar4_recv.at[slot],
            send_sem=a4_ssem.at[n],
            recv_sem=a4_rsem.at[slot],
            device_id={"space": s, "member": member},
        )

    def totals_out(d, _):
        n = lax.rem(m + d, MEMBER)
        copy_a4(n, m, n).start()
        return 0

    lax.fori_loop(1, MEMBER, totals_out, 0)
    total[:, pl.ds(pl.multiple_of(128 * m, 128), 128)] = final.astype(BF16).astype(F32)

    def totals_in(d, _):
        n = lax.rem(m + MEMBER - d, MEMBER)
        copy_a4(n, n, n).wait_recv()
        total[:, pl.ds(pl.multiple_of(128 * n, 128), 128)] = ar4_recv[n].astype(F32)
        return 0

    lax.fori_loop(1, MEMBER, totals_in, 0)
    for k in range(KW * KW):
        base, off = CP * k // 128 * 128, CP * k % 128
        width = 256 if off else 128
        part = total[0:CH, base : base + width]
        if off:
            part = pltpu.roll(part, width - off, 1)
        kgrad_ref[k] = part[:, 0:CH]

    def sent(d, _):
        n = lax.rem(m + d, MEMBER)
        copy1(n, m, n).wait_send()
        copy2(1, n, m, s, n).wait_send()
        copy_a1(n, m, n).wait_send()
        copy_a4(n, m, n).wait_send()
        return 0

    lax.fori_loop(1, MEMBER, sent, 0)

    def halo_sent(d, _):
        n = lax.rem(m + d, MEMBER)

        @pl.when(has_prev)
        def _():
            copy2(2, n, m, s - 1, n).wait_send()

        @pl.when(has_next)
        def _():
            copy2(0, n, m, s + 1, n).wait_send()

        return 0

    lax.fori_loop(0, MEMBER, halo_sent, 0)

    def tiles_sent(j, _):
        t = reducer_of(j, m)

        @pl.when(t != s)
        def _():
            copy_a2(j, s, t).wait_send()

        return 0

    lax.fori_loop(0, TILES, tiles_sent, 0)

    @pl.when(reducing)
    def _():
        def one(d, _):
            t = lax.rem(s + d, SPACE)
            copy_a3(mine, t, t).wait_send()
            return 0

        lax.fori_loop(1, SPACE, one, 0)


def call(weights, pred, truth, scale, hidden, filters):
    vmem = pl.BlockSpec(memory_space=pltpu.VMEM)
    dma = pltpu.SemaphoreType.DMA
    return pl.pallas_call(
        kernel,
        out_shape=(
            jax.ShapeDtypeStruct((2, CH, LON), BF16),
            jax.ShapeDtypeStruct((KW * KW, CH, CH), F32),
        ),
        in_specs=[pl.BlockSpec(memory_space=pltpu.SMEM)] + [vmem] * 5,
        out_specs=(vmem, vmem),
        scratch_shapes=[
            pltpu.VMEM((MEMBER, PK, 128), BF16),
            pltpu.VMEM((MEMBER, PK, 128), BF16),
            pltpu.VMEM((MEMBER, PK, 128), F32),
            pltpu.VMEM((CH, 256), F32),
            pltpu.VMEM((CP, 128), F32),
            pltpu.VMEM((MEMBER, PK, 128), BF16),
            pltpu.VMEM((3, MEMBER, PK, 128), BF16),
            pltpu.VMEM((CP, LP), F32),
            pltpu.VMEM((6 * KC, LP), BF16),
            pltpu.VMEM((6, 2 * CP, 512), BF16),
            pltpu.VMEM((KW, CP, 512), F32),
            pltpu.VMEM((CP, 2048), F32),
            pltpu.VMEM((2 * CP, LP), F32),
            pltpu.VMEM((MEMBER, CP, 128), BF16),
            pltpu.VMEM((MEMBER, CP, 128), BF16),
            pltpu.VMEM((TILES, 8, 128), F32),
            pltpu.VMEM((SPACE, 8, 128), F32),
            pltpu.VMEM((8, 128), F32),
            pltpu.VMEM((TILES, 8, 128), F32),
            pltpu.VMEM((CP, 128), BF16),
            pltpu.VMEM((MEMBER, CP, 128), BF16),
            dma((MEMBER,)),
            dma((MEMBER,)),
            dma((3, MEMBER)),
            dma((3, MEMBER)),
            dma((MEMBER,)),
            dma((MEMBER,)),
            dma((TILES,)),
            dma((SPACE,)),
            dma((SPACE,)),
            dma((TILES,)),
            dma((MEMBER,)),
            dma((MEMBER,)),
        ],
        compiler_params=pltpu.CompilerParams(
            collective_id=0, has_side_effects=True, vmem_limit_bytes=48 * 1024 * 1024
        ),
    )(weights, pred, truth, scale, hidden, filters)


def body(prediction_maps, truth_analysis, reciprocal_spread, deconv_inputs, filter_tensor):
    rows = 2 * SPACE
    index = np.arange(rows, dtype=np.float64)
    cosine = np.cos((index + 0.5) * (np.pi / rows) - np.pi / 2)
    weights = jnp.asarray((cosine / cosine.mean()).astype(np.float32))
    pred = jnp.pad(jnp.transpose(prediction_maps[0], (1, 0, 2)), ((0, 0), (0, 0), (0, LP - LON)))
    hidden = jnp.pad(
        jnp.transpose(deconv_inputs[0], (1, 0, 2)), ((0, 0), (0, CP - CH), (0, LP - LON))
    ).reshape(2 * CP, LP)
    back, kgrad = call(
        weights, pred, truth_analysis, reciprocal_spread.reshape(1, CH), hidden, filter_tensor
    )
    return jnp.transpose(back, (1, 0, 2))[None], kgrad.reshape(KW, KW, CH, CH)


def solution(mesh):
    return jax.shard_map(
        body,
        mesh=mesh,
        in_specs=(
            P("member", None, "space", None),
            P(None, ("space", "member")),
            P(),
            P("member", None, "space", None),
            P(),
        ),
        out_specs=(P("member", None, "space", None), P()),
        check_vma=False,
    )
```

```python
import functools

import jax
import jax.numpy as jnp
import numpy as np
from jax import lax
from jax.experimental import pallas as pl
from jax.experimental.pallas import tpu as pltpu
from jax.sharding import PartitionSpec as P

F32 = jnp.float32
BF16 = jnp.bfloat16
SPACE = 32
MEMBER = 16
CH = 72
CP = 80
LON = 1440
LP = 1536
PX = 180
KW = 5
KC = KW * CH
KP = 368
PK = 112
SHARES = 27
SR = 40


def lane_index(rows):
    return lax.broadcasted_iota(jnp.int32, (rows, 128), 1)


def packed(wide):
    lane = lane_index(40)
    rest = wide[:, 128:256]
    low = rest[0:40]
    high = jnp.concatenate([rest[40:72], jnp.zeros((8, 128), F32)], axis=0)
    low = jnp.where(lane < PX - 128, low, 0.0)
    high = jnp.where(lane < PX - 128, high, 0.0)
    tail = jnp.where(lane < 64, low, pltpu.roll(high, 64, 1))
    return jnp.concatenate([wide[:, 0:128], tail], axis=0)


def kernel(
    weight_ref,
    pred_ref,
    truth_ref,
    scale_ref,
    hidden_ref,
    filter_ref,
    back_ref,
    kgrad_ref,
    send1,
    recv1,
    scaled,
    trscr,
    fscr,
    send2,
    recv2,
    hid,
    ext,
    stack,
    wst,
    total,
    out_acc,
    ar1_send,
    ar1_recv,
    z1_send,
    z1_recv,
    z2_send,
    z2_recv,
    ar4_send,
    ar4_recv,
    s1_sem,
    r1_sem,
    h1_ssem,
    h1_rsem,
    h2_ssem,
    h2_rsem,
    s2_sem,
    r2_sem,
    a1_ssem,
    a1_rsem,
    z1_ssem,
    z1_rsem,
    z2_ssem,
    z2_rsem,
    a4_ssem,
    a4_rsem,
    near_sem,
    far_sem,
):
    s = lax.axis_index("space")
    m = lax.axis_index("member")
    side = lax.rem(s, 2)
    even = side == 0
    partner = s + 1 - 2 * side
    beyond = s + 2 - 4 * side
    has_prev = s > 0
    has_next = s < SPACE - 1
    has_beyond = jnp.logical_and(beyond >= 0, beyond < SPACE)
    share_id = MEMBER * side + m
    holds_share = share_id < SHARES

    def band(k):
        return lax.rem(s + SPACE + k, SPACE)

    z_low = lax.rem(s // 2, 4)
    z_high = s // 8

    def block_mate(k):
        return 8 * z_high + 2 * lax.rem(z_low + k, 4) + side

    def comb_mate(k):
        return 8 * lax.rem(z_high + k, 4) + 2 * z_low + side

    barrier = pltpu.get_barrier_semaphore()

    def greet(space, member):
        pl.semaphore_signal(barrier, inc=1, device_id={"space": space, "member": member})

    def greet_members(d, _):
        greet(s, lax.rem(m + d, MEMBER))
        return 0

    lax.fori_loop(1, MEMBER, greet_members, 0)

    def greet_bands(d, _):
        n = lax.rem(m + d, MEMBER)

        @pl.when(has_prev)
        def _():
            greet(s - 1, n)

        @pl.when(has_next)
        def _():
            greet(s + 1, n)

        return 0

    lax.fori_loop(0, MEMBER, greet_bands, 0)
    for k in (4, -4):
        greet(band(k), m)
    for k in (1, 2, 3):
        greet(block_mate(k), m)
    pl.semaphore_wait(
        barrier, MEMBER + 4 + jnp.where(has_prev, MEMBER, 0) + jnp.where(has_next, MEMBER, 0)
    )

    def copy1(src, slot, member):
        return pltpu.make_async_remote_copy(
            src_ref=send1.at[src],
            dst_ref=recv1.at[slot],
            send_sem=s1_sem.at[src],
            recv_sem=r1_sem.at[slot],
            device_id={"space": s, "member": member},
        )

    def fields_out(d, _):
        n = lax.rem(m + d, MEMBER)
        row = n // 8
        start = PX * lax.rem(n, 8)
        off = lax.rem(start, 128)
        base = pl.multiple_of(start - off, 128)
        window = pred_ref[row, :, pl.ds(base, 384)].astype(F32)
        wide = pltpu.roll(window, lax.rem(384 - off, 384), 1)[:, 0:256]
        chunk = packed(wide).astype(BF16)

        @pl.when(d < MEMBER)
        def _():
            send1[n] = chunk
            copy1(n, m, n).start()

        @pl.when(d == MEMBER)
        def _():
            recv1[n] = chunk

        return 0

    lax.fori_loop(1, MEMBER + 1, fields_out, 0)

    near_at = 4 - 4 * side
    far_at = 4 * side
    far_at_beyond = 4 * side

    def hidden_near(r, at):
        return pltpu.make_async_remote_copy(
            src_ref=hidden_ref.at[r],
            dst_ref=hid.at[at + r],
            send_sem=h1_ssem.at[r],
            recv_sem=h1_rsem.at[r],
            device_id={"space": partner, "member": m},
        )

    def hidden_far(r, src, dst):
        return pltpu.make_async_remote_copy(
            src_ref=hid.at[src + r],
            dst_ref=hid.at[dst + r],
            send_sem=h2_ssem.at[r],
            recv_sem=h2_rsem.at[r],
            device_id={"space": beyond, "member": m},
        )

    for r in range(2):
        hidden_near(r, far_at).start()
    for k in (4, -4):
        pl.semaphore_signal(near_sem, inc=1, device_id={"space": band(k), "member": m})

    eye = lax.broadcasted_iota(jnp.int32, (CH, CH), 0) == lax.broadcasted_iota(jnp.int32, (CH, CH), 1)
    scale_col = jnp.sum(jnp.where(eye, scale_ref[...], 0.0), axis=1, keepdims=True)
    scale_wide = jnp.broadcast_to(scale_col, (CH, 128))
    scale_pk = packed(jnp.concatenate([scale_wide, scale_wide], axis=1))
    trscr[...] = jnp.zeros_like(trscr)
    trscr[:, 0:PX] = truth_ref[...]
    truth_pk = packed(trscr[...])

    fscr[...] = jnp.zeros_like(fscr)
    wst[...] = jnp.zeros_like(wst)
    for a in range(KW):
        acc = None
        for b in range(KW):
            fscr[0:CH, 0:CH] = filter_ref[a, b].astype(F32)
            part = jnp.concatenate([fscr[...], jnp.zeros((CP, 256), F32)], axis=1)
            if b:
                part = pltpu.roll(part, CH * b, 1)
            acc = part if acc is None else acc + part
        acc = acc.astype(BF16)
        wst[a, 0:CP, :] = acc
        wst[a + 1, CP : 2 * CP, :] = acc
    out_acc[...] = jnp.zeros_like(out_acc)
    for r in range(2):
        hid[2 + r] = hidden_ref[r]

    @pl.when(jnp.logical_not(has_prev))
    def _():
        hid[0] = jnp.zeros((CP, LP), BF16)
        hid[1] = jnp.zeros((CP, LP), BF16)

    @pl.when(jnp.logical_not(has_next))
    def _():
        hid[4] = jnp.zeros((CP, LP), BF16)
        hid[5] = jnp.zeros((CP, LP), BF16)

    def fields_in(d, _):
        n = lax.rem(m + MEMBER - d, MEMBER)

        @pl.when(d < MEMBER)
        def _():
            copy1(n, n, n).wait_recv()

        scaled[n] = scale_pk * recv1[n].astype(F32)
        return 0

    lax.fori_loop(1, MEMBER + 1, fields_in, 0)

    weight = weight_ref[2 * s + m // 8]

    def copy2(kind, src, slot, space, member):
        return pltpu.make_async_remote_copy(
            src_ref=send2.at[src],
            dst_ref=recv2.at[kind, slot],
            send_sem=s2_sem.at[kind, src],
            recv_sem=r2_sem.at[kind, slot],
            device_id={"space": space, "member": member},
        )

    def column_sums(square):
        main = jnp.sum(square[0:CH], axis=0, keepdims=True)
        tail = jnp.sum(square[CH:PK], axis=0, keepdims=True)
        return main, tail + pltpu.roll(tail, 64, 1)

    def spread_out(main, tail):
        return jnp.concatenate(
            [jnp.broadcast_to(main, (CH, 128)), jnp.broadcast_to(tail, (PK - CH, 128))], axis=0
        )

    def gradient(d, _):
        n = lax.rem(m + d, MEMBER)
        y = scaled[n]
        offset = scale_pk * (recv1[n].astype(F32) - truth_pk)
        main, tail = column_sums(offset * offset)
        direct = scale_pk * offset * spread_out(lax.rsqrt(main + 1.0), lax.rsqrt(tail + 1.0))

        def pair(k, mix):
            diff = scaled[k] - y
            main, tail = column_sums(diff * diff)
            return mix + diff * spread_out(lax.rsqrt(main + 1.0), lax.rsqrt(tail + 1.0))

        mix = lax.fori_loop(0, MEMBER, pair, jnp.zeros((PK, 128), F32), unroll=4)
        grad = (weight * (direct + scale_pk * mix * (1.0 / MEMBER))).astype(BF16)
        send2[n] = grad

        @pl.when(d < MEMBER)
        def _():
            copy2(1, n, m, s, n).start()

        @pl.when(d == MEMBER)
        def _():
            recv2[1, n] = grad

        for r in range(2):

            @pl.when(d == 4 + 6 * r)
            def _():
                hidden_near(r, near_at).wait_recv()

                @pl.when(has_beyond)
                def _():
                    hidden_far(r, near_at, far_at_beyond).start()

        return 0

    lax.fori_loop(1, MEMBER + 1, gradient, 0)
    pl.semaphore_wait(near_sem, 2)
    for k in (8, -8):
        pl.semaphore_signal(far_sem, inc=1, device_id={"space": band(k), "member": m})

    def halo_prev(d, _):
        n = lax.rem(m + d, MEMBER)

        @pl.when(has_prev)
        def _():
            copy2(2, n, m, s - 1, n).start()

        return 0

    def halo_next(d, _):
        n = lax.rem(m + d, MEMBER)

        @pl.when(has_next)
        def _():
            copy2(0, n, m, s + 1, n).start()

        return 0

    lax.fori_loop(0, MEMBER, halo_next, 0)
    lax.fori_loop(0, MEMBER, halo_prev, 0)

    def wait_block(kind):
        def one(d, _):
            n = lax.rem(m + MEMBER - d, MEMBER)

            @pl.when(jnp.logical_or(kind != 1, d > 0))
            def _():
                copy2(kind, n, n, s, n).wait_recv()

            return 0

        lax.fori_loop(0, MEMBER, one, 0)

    def rows_ready(kind, half):
        q = 2 * kind + half
        ext[...] = jnp.zeros_like(ext)
        lane = lane_index(PK - CH)
        for k in range(8):
            chunk = recv2[kind, 8 * half + k].astype(F32)
            tail = chunk[CH:PK]
            low = jnp.where(lane < PX - 128, tail, 0.0)
            high = jnp.where(lane < PX - 128, pltpu.roll(tail, 64, 1), 0.0)
            rest = jnp.concatenate([low, high[0:32]], axis=0)
            wide = jnp.concatenate([chunk[0:CH], rest, jnp.zeros((CH, 128), F32)], axis=1)
            start = PX * k + 2
            base, off = start // 128 * 128, start % 128
            ext[:, base : base + 384] += pltpu.roll(wide, off, 1)
        first = ext[:, 0:128]
        last = ext[:, LP - 128 : LP]
        lane = lane_index(CH)
        ext[:, 0:128] = jnp.where(lane < 2, pltpu.roll(last, 96, 1), first)
        ext[:, LP - 128 : LP] = jnp.where(
            jnp.logical_and(lane >= 34, lane < 36), pltpu.roll(first, 32, 1), last
        )

        def piece(p):
            b, g = p // 9, p % 9
            if b == KW:
                return jnp.zeros((8, LP), F32)
            rows = ext[8 * g : 8 * g + 8, :]
            return pltpu.roll(rows, LP - b, 1) if b else rows

        for k in range(KP // 16):
            both = jnp.concatenate([piece(2 * k), piece(2 * k + 1)], axis=0)
            stack[q, 16 * k : 16 * k + 16, :] = both.astype(BF16)

    def block_rows(kind):
        def one(half, _):
            rows_ready(kind, half)
            return 0

        lax.fori_loop(0, 2, one, 0)

    def hidden_terms(kind):
        def one(half, _):
            q = 2 * kind + half
            out_acc[...] += jnp.dot(wst[q, :, 0:KP], stack[q], preferred_element_type=F32)
            return 0

        lax.fori_loop(0, 2, one, 0)

    wait_block(1)
    block_rows(1)

    from_beyond = s - 2 + 4 * side
    has_from = jnp.logical_and(from_beyond >= 0, from_beyond < SPACE)

    @pl.when(has_from)
    def _():
        for r in range(2):
            hidden_far(r, 0, 4 * side).wait_recv()

    def kernel_terms(half):
        rows = hid[half : half + KW].reshape(KW * CP, LP)
        return lax.dot_general(
            rows, stack[2 + half], (((1,), (1,)), ((), ())), preferred_element_type=F32
        )

    product = kernel_terms(0) + kernel_terms(1)
    total[...] = jnp.zeros_like(total)
    for t in range(KW):
        total[CH * t : CH * t + CH, 0:KP] = product[CP * t : CP * t + CH]

    def share_rows(u):
        return pl.ds(pl.multiple_of(SR * lax.rem(u, 9), 8), SR)

    def share_lanes(u):
        return pl.ds(pl.multiple_of(128 * (u // 9), 128), 128)

    def copy_a1(src, slot, space, member):
        return pltpu.make_async_remote_copy(
            src_ref=ar1_send.at[src],
            dst_ref=ar1_recv.at[slot],
            send_sem=a1_ssem.at[src],
            recv_sem=a1_rsem.at[slot],
            device_id={"space": space, "member": member},
        )

    def share_owner(u):
        return s - side + u // MEMBER, lax.rem(u, MEMBER)

    def shares_out(d, _):
        u = lax.rem(share_id + d, 2 * MEMBER)

        @pl.when(u < SHARES)
        def _():
            ar1_send[u] = total[share_rows(u), share_lanes(u)].astype(BF16)
            space, member = share_owner(u)
            copy_a1(u, share_id, space, member).start()

        return 0

    lax.fori_loop(1, 2 * MEMBER, shares_out, 0)

    hidden_terms(1)

    def z1(k, slot):
        return pltpu.make_async_remote_copy(
            src_ref=z1_send,
            dst_ref=z1_recv.at[slot],
            send_sem=z1_ssem.at[k],
            recv_sem=z1_rsem.at[slot],
            device_id={"space": block_mate(k), "member": m},
        )

    def z2(k, slot):
        return pltpu.make_async_remote_copy(
            src_ref=z2_send,
            dst_ref=z2_recv.at[slot],
            send_sem=z2_ssem.at[k],
            recv_sem=z2_rsem.at[slot],
            device_id={"space": comb_mate(k), "member": m},
        )

    pl.semaphore_wait(far_sem, 2)

    @pl.when(holds_share)
    def _():
        def shares_in(d, acc):
            u = lax.rem(share_id + 2 * MEMBER - d, 2 * MEMBER)
            space, member = share_owner(u)
            copy_a1(0, u, space, member).wait_recv()
            return acc + ar1_recv[u].astype(F32)

        own = total[share_rows(share_id), share_lanes(share_id)]
        acc = lax.fori_loop(1, 2 * MEMBER, shares_in, own)
        z1_send[...] = acc
        z1_recv[z_low] = acc
        for k in (1, 2, 3):
            z1(k, z_low).start()

    @pl.when(has_prev)
    def _():
        wait_block(0)
        block_rows(0)
        hidden_terms(0)

    @pl.when(holds_share)
    def _():
        for k in (1, 2, 3):
            z1(k, lax.rem(z_low + k, 4)).wait_recv()
        acc = (z1_recv[0] + z1_recv[1]) + (z1_recv[2] + z1_recv[3])
        z2_send[...] = acc
        z2_recv[z_high] = acc
        for k in (1, 2, 3):
            z2(k, z_high).start()

    @pl.when(has_next)
    def _():
        wait_block(2)
        block_rows(2)
        hidden_terms(2)

    norm = float(1.0 / np.sqrt(np.float32(MEMBER * 2 * SPACE * LON)))

    def copy_a4(u, slot, space, member):
        return pltpu.make_async_remote_copy(
            src_ref=ar4_send,
            dst_ref=ar4_recv.at[slot],
            send_sem=a4_ssem.at[u],
            recv_sem=a4_rsem.at[slot],
            device_id={"space": space, "member": member},
        )

    @pl.when(holds_share)
    def _():
        for k in (1, 2, 3):
            z2(k, lax.rem(z_high + k, 4)).wait_recv()
        acc = (z2_recv[0] + z2_recv[1]) + (z2_recv[2] + z2_recv[3])
        final = (acc * norm).astype(BF16)
        ar4_send[...] = final
        total[share_rows(share_id), share_lanes(share_id)] = final.astype(F32)

        def totals_out(d, _):
            u = lax.rem(share_id + d, 2 * MEMBER)
            space, member = share_owner(u)
            copy_a4(u, share_id, space, member).start()
            return 0

        lax.fori_loop(1, 2 * MEMBER, totals_out, 0)

    back_ref[0] = out_acc[0:CH, 0:LON].astype(BF16)
    back_ref[1] = out_acc[CP : CP + CH, 0:LON].astype(BF16)

    def totals_in(d, _):
        u = lax.rem(share_id + 2 * MEMBER - d, 2 * MEMBER)

        @pl.when(u < SHARES)
        def _():
            space, member = share_owner(u)
            copy_a4(0, u, space, member).wait_recv()
            total[share_rows(u), share_lanes(u)] = ar4_recv[u].astype(F32)

        return 0

    lax.fori_loop(1, 2 * MEMBER, totals_in, 0)
    for a in range(KW):
        for b in range(KW):
            base, off = CH * b // 128 * 128, CH * b % 128
            width = 256 if off + CH > 128 else 128
            part = total[CH * (4 - a) : CH * (5 - a), base : base + width]
            if off:
                part = pltpu.roll(part, width - off, 1)
            kgrad_ref[KW * a + b] = part[:, 0:CH]

    def sent(d, _):
        n = lax.rem(m + d, MEMBER)
        copy1(n, m, n).wait_send()
        copy2(1, n, m, s, n).wait_send()
        return 0

    lax.fori_loop(1, MEMBER, sent, 0)

    def halo_sent(d, _):
        n = lax.rem(m + d, MEMBER)

        @pl.when(has_prev)
        def _():
            copy2(2, n, m, s - 1, n).wait_send()

        @pl.when(has_next)
        def _():
            copy2(0, n, m, s + 1, n).wait_send()

        return 0

    lax.fori_loop(0, MEMBER, halo_sent, 0)

    def shares_sent(d, _):
        u = lax.rem(share_id + d, 2 * MEMBER)
        space, member = share_owner(u)

        @pl.when(u < SHARES)
        def _():
            copy_a1(u, share_id, space, member).wait_send()

        @pl.when(holds_share)
        def _():
            copy_a4(u, share_id, space, member).wait_send()

        return 0

    lax.fori_loop(1, 2 * MEMBER, shares_sent, 0)
    for r in range(2):
        hidden_near(r, far_at).wait_send()

        @pl.when(has_beyond)
        def _():
            hidden_far(r, near_at, far_at_beyond).wait_send()

    @pl.when(holds_share)
    def _():
        for k in (1, 2, 3):
            z1(k, z_low).wait_send()
            z2(k, z_high).wait_send()


def call(weights, pred, truth, scale, hidden, filters):
    vmem = pl.BlockSpec(memory_space=pltpu.VMEM)
    dma = pltpu.SemaphoreType.DMA
    return pl.pallas_call(
        kernel,
        out_shape=(
            jax.ShapeDtypeStruct((2, CH, LON), BF16),
            jax.ShapeDtypeStruct((KW * KW, CH, CH), F32),
        ),
        in_specs=[pl.BlockSpec(memory_space=pltpu.SMEM)] + [vmem] * 5,
        out_specs=(vmem, vmem),
        scratch_shapes=[
            pltpu.VMEM((MEMBER, PK, 128), BF16),
            pltpu.VMEM((MEMBER, PK, 128), BF16),
            pltpu.VMEM((MEMBER, PK, 128), F32),
            pltpu.VMEM((CH, 256), F32),
            pltpu.VMEM((CP, 128), F32),
            pltpu.VMEM((MEMBER, PK, 128), BF16),
            pltpu.VMEM((3, MEMBER, PK, 128), BF16),
            pltpu.VMEM((6, CP, LP), BF16),
            pltpu.VMEM((CH, LP), F32),
            pltpu.VMEM((6, KP, LP), BF16),
            pltpu.VMEM((6, 2 * CP, 384), BF16),
            pltpu.VMEM((KC, 384), F32),
            pltpu.VMEM((2 * CP, LP), F32),
            pltpu.VMEM((2 * MEMBER, SR, 128), BF16),
            pltpu.VMEM((2 * MEMBER, SR, 128), BF16),
            pltpu.VMEM((SR, 128), F32),
            pltpu.VMEM((4, SR, 128), F32),
            pltpu.VMEM((SR, 128), F32),
            pltpu.VMEM((4, SR, 128), F32),
            pltpu.VMEM((SR, 128), BF16),
            pltpu.VMEM((2 * MEMBER, SR, 128), BF16),
            dma((MEMBER,)),
            dma((MEMBER,)),
            dma((2,)),
            dma((2,)),
            dma((2,)),
            dma((2,)),
            dma((3, MEMBER)),
            dma((3, MEMBER)),
            dma((2 * MEMBER,)),
            dma((2 * MEMBER,)),
            dma((4,)),
            dma((4,)),
            dma((4,)),
            dma((4,)),
            dma((2 * MEMBER,)),
            dma((2 * MEMBER,)),
            pltpu.SemaphoreType.REGULAR,
            pltpu.SemaphoreType.REGULAR,
        ],
        compiler_params=pltpu.CompilerParams(
            collective_id=0, has_side_effects=True, vmem_limit_bytes=48 * 1024 * 1024
        ),
    )(weights, pred, truth, scale, hidden, filters)


def body(prediction_maps, truth_analysis, reciprocal_spread, deconv_inputs, filter_tensor):
    rows = 2 * SPACE
    index = np.arange(rows, dtype=np.float64)
    cosine = np.cos((index + 0.5) * (np.pi / rows) - np.pi / 2)
    weights = jnp.asarray((cosine / cosine.mean()).astype(np.float32))
    pred = jnp.pad(jnp.transpose(prediction_maps[0], (1, 0, 2)), ((0, 0), (0, 0), (0, LP - LON)))
    hidden = jnp.pad(
        jnp.transpose(deconv_inputs[0], (1, 0, 2)), ((0, 0), (0, CP - CH), (0, LP - LON))
    )
    back, kgrad = call(
        weights, pred, truth_analysis, reciprocal_spread.reshape(1, CH), hidden, filter_tensor
    )
    return jnp.transpose(back, (1, 0, 2))[None], kgrad.reshape(KW, KW, CH, CH)


def solution(mesh):
    return jax.shard_map(
        body,
        mesh=mesh,
        in_specs=(
            P("member", None, "space", None),
            P(None, ("space", "member")),
            P(),
            P("member", None, "space", None),
            P(),
        ),
        out_specs=(P("member", None, "space", None), P()),
        check_vma=False,
    )
```

```python
import functools

import jax
import jax.numpy as jnp
import numpy as np
from jax import lax
from jax.experimental import pallas as pl
from jax.experimental.pallas import tpu as pltpu
from jax.sharding import PartitionSpec as P

F32 = jnp.float32
BF16 = jnp.bfloat16
SPACE = 32
MEMBER = 16
CH = 72
CP = 80
LON = 1440
LP = 1536
PX = 180
KW = 5
KC = KW * CH
KP = 368
PK = 112
SHARES = 27
SR = 40


def lane_index(rows):
    return lax.broadcasted_iota(jnp.int32, (rows, 128), 1)


def packed(wide):
    lane = lane_index(40)
    rest = wide[:, 128:256]
    low = rest[0:40]
    high = jnp.concatenate([rest[40:72], jnp.zeros((8, 128), F32)], axis=0)
    low = jnp.where(lane < PX - 128, low, 0.0)
    high = jnp.where(lane < PX - 128, high, 0.0)
    tail = jnp.where(lane < 64, low, pltpu.roll(high, 64, 1))
    return jnp.concatenate([wide[:, 0:128], tail], axis=0)


def kernel(
    weight_ref,
    pred_ref,
    truth_ref,
    scale_ref,
    hidden_ref,
    filter_ref,
    back_ref,
    kgrad_ref,
    send1,
    recv1,
    scaled,
    target,
    factor,
    grads,
    trscr,
    fscr,
    send2,
    recv2,
    hid,
    ext,
    stack,
    wst,
    total,
    out_acc,
    ar1_send,
    ar1_recv,
    z1_send,
    z1_recv,
    z2_send,
    z2_recv,
    ar4_send,
    ar4_recv,
    s1_sem,
    r1_sem,
    h1_ssem,
    h1_rsem,
    h2_ssem,
    h2_rsem,
    s2_sem,
    r2_sem,
    a1_ssem,
    a1_rsem,
    z1_ssem,
    z1_rsem,
    z2_ssem,
    z2_rsem,
    a4_ssem,
    a4_rsem,
    span1,
    span2,
    span4,
    span8,
):
    s = lax.axis_index("space")
    m = lax.axis_index("member")
    side = lax.rem(s, 2)
    even = side == 0
    partner = s + 1 - 2 * side
    beyond = s + 2 - 4 * side
    has_prev = s > 0
    has_next = s < SPACE - 1
    has_beyond = jnp.logical_and(beyond >= 0, beyond < SPACE)
    share_id = MEMBER * side + m
    holds_share = share_id < SHARES

    def band(k):
        return lax.rem(s + SPACE + k, SPACE)

    z_low = lax.rem(s // 2, 4)
    z_high = s // 8

    def block_mate(k):
        return 8 * z_high + 2 * lax.rem(z_low + k, 4) + side

    def comb_mate(k):
        return 8 * lax.rem(z_high + k, 4) + 2 * z_low + side

    barrier = pltpu.get_barrier_semaphore()

    def greet(space, member):
        pl.semaphore_signal(barrier, inc=1, device_id={"space": space, "member": member})

    def greet_members(d, _):
        greet(s, lax.rem(m + d, MEMBER))
        return 0

    lax.fori_loop(1, MEMBER, greet_members, 0)

    for k in (1, -1):
        greet(band(k), m)
    pl.semaphore_wait(barrier, MEMBER + 1)

    def tell(sem, k):
        for offset in (k, -k):
            pl.semaphore_signal(sem, inc=1, device_id={"space": band(offset), "member": m})

    tell(span1, 1)

    def copy1(src, slot, member):
        return pltpu.make_async_remote_copy(
            src_ref=send1.at[src],
            dst_ref=recv1.at[slot],
            send_sem=s1_sem.at[src],
            recv_sem=r1_sem.at[slot],
            device_id={"space": s, "member": member},
        )

    def fields_out(d, _):
        n = lax.rem(m + d, MEMBER)
        row = n // 8
        start = PX * lax.rem(n, 8)
        off = lax.rem(start, 128)
        base = pl.multiple_of(start - off, 128)
        window = pred_ref[row, :, pl.ds(base, 384)].astype(F32)
        wide = pltpu.roll(window, lax.rem(384 - off, 384), 1)[:, 0:256]
        chunk = packed(wide).astype(BF16)

        @pl.when(d < MEMBER)
        def _():
            send1[n] = chunk
            copy1(n, m, n).start()

        @pl.when(d == MEMBER)
        def _():
            recv1[n] = chunk

        return 0

    lax.fori_loop(1, MEMBER + 1, fields_out, 0)

    near_at = 4 - 4 * side
    far_at = 4 * side
    far_at_beyond = 4 * side

    def hidden_near(r, at):
        return pltpu.make_async_remote_copy(
            src_ref=hidden_ref.at[r],
            dst_ref=hid.at[at + r],
            send_sem=h1_ssem.at[r],
            recv_sem=h1_rsem.at[r],
            device_id={"space": partner, "member": m},
        )

    def hidden_far(r, src, dst):
        return pltpu.make_async_remote_copy(
            src_ref=hid.at[src + r],
            dst_ref=hid.at[dst + r],
            send_sem=h2_ssem.at[r],
            recv_sem=h2_rsem.at[r],
            device_id={"space": beyond, "member": m},
        )

    for r in range(2):
        hidden_near(r, far_at).start()

    eye = lax.broadcasted_iota(jnp.int32, (CH, CH), 0) == lax.broadcasted_iota(jnp.int32, (CH, CH), 1)
    scale_col = jnp.sum(jnp.where(eye, scale_ref[...], 0.0), axis=1, keepdims=True)
    scale_wide = jnp.broadcast_to(scale_col, (CH, 128))
    scale_pk = packed(jnp.concatenate([scale_wide, scale_wide], axis=1))
    trscr[...] = jnp.zeros_like(trscr)
    trscr[:, 0:PX] = truth_ref[...]
    truth_pk = packed(trscr[...])

    fscr[...] = jnp.zeros_like(fscr)
    wst[...] = jnp.zeros_like(wst)
    for a in range(KW):
        acc = None
        for b in range(KW):
            fscr[0:CH, 0:CH] = filter_ref[a, b].astype(F32)
            part = jnp.concatenate([fscr[...], jnp.zeros((CP, 256), F32)], axis=1)
            if b:
                part = pltpu.roll(part, CH * b, 1)
            acc = part if acc is None else acc + part
        acc = acc.astype(BF16)
        wst[a, 0:CP, :] = acc
        wst[a + 1, CP : 2 * CP, :] = acc
    out_acc[...] = jnp.zeros_like(out_acc)
    for r in range(2):
        hid[2 + r] = hidden_ref[r]

    @pl.when(jnp.logical_not(has_prev))
    def _():
        hid[0] = jnp.zeros((CP, LP), BF16)
        hid[1] = jnp.zeros((CP, LP), BF16)

    @pl.when(jnp.logical_not(has_next))
    def _():
        hid[4] = jnp.zeros((CP, LP), BF16)
        hid[5] = jnp.zeros((CP, LP), BF16)

    pl.semaphore_wait(span1, 2)
    tell(span2, 2)

    def fields_in(d, _):
        n = lax.rem(m + MEMBER - d, MEMBER)

        @pl.when(d < MEMBER)
        def _():
            copy1(n, n, n).wait_recv()

        y = scale_pk * recv1[n].astype(F32)
        scaled[pl.ds(n, PK, stride=2 * MEMBER), :] = y
        scaled[pl.ds(n + MEMBER, PK, stride=2 * MEMBER), :] = y
        return 0

    lax.fori_loop(1, MEMBER + 1, fields_in, 0)
    pl.semaphore_wait(span2, 2)
    tell(span4, 4)

    target[...] = scale_pk * truth_pk
    factor[...] = weight_ref[2 * s + m // 8] * scale_pk
    turns = MEMBER // 2

    def fields_of(c, turn):
        return scaled[pl.ds(2 * MEMBER * c + turn, MEMBER), :]

    def squares(c, sums):
        y = fields_of(c, 0)
        off = y - target[pl.ds(c, 1), :]
        new = [sums[0] + off * off]
        for r in range(1, turns + 1):
            diff = fields_of(c, r) - y
            new.append(sums[r] + diff * diff)
        return tuple(new)

    zeros = tuple(jnp.zeros((MEMBER, 128), F32) for _ in range(turns + 1))
    main_sums = lax.fori_loop(0, CH, squares, zeros, unroll=4)
    tail_sums = lax.fori_loop(CH, PK, squares, zeros, unroll=4)

    def inverses(sums, tail):
        inv = []
        for v in sums:
            if tail:
                v = v + pltpu.roll(v, 64, 1)
            inv.append(lax.rsqrt(v + 1.0))
        for r in range(turns + 1, MEMBER):
            inv.append(pltpu.roll(inv[MEMBER - r], MEMBER - r, 0))
        return inv

    def mixtures(inv):
        all_of = functools.reduce(lambda a, b: a + b, inv[1:])

        def one(c, _):
            y = fields_of(c, 0)
            mix = inv[1] * fields_of(c, 1)
            for r in range(2, MEMBER):
                mix = mix + inv[r] * fields_of(c, r)
            direct = (y - target[pl.ds(c, 1), :]) * inv[0]
            value = direct + (mix - y * all_of) * (1.0 / MEMBER)
            grads[pl.ds(MEMBER * c, MEMBER), :] = value * factor[pl.ds(c, 1), :]
            return 0

        return one

    lax.fori_loop(0, CH, mixtures(inverses(main_sums, False)), 0, unroll=4)
    lax.fori_loop(CH, PK, mixtures(inverses(tail_sums, True)), 0, unroll=4)

    def copy2(kind, src, slot, space, member):
        return pltpu.make_async_remote_copy(
            src_ref=send2.at[src],
            dst_ref=recv2.at[kind, slot],
            send_sem=s2_sem.at[kind, src],
            recv_sem=r2_sem.at[kind, slot],
            device_id={"space": space, "member": member},
        )

    def gradients_out(d, _):
        n = lax.rem(m + d, MEMBER)
        grad = grads[pl.ds(n, PK, stride=MEMBER), :].astype(BF16)
        send2[n] = grad

        @pl.when(d < MEMBER)
        def _():
            copy2(1, n, m, s, n).start()

        @pl.when(d == MEMBER)
        def _():
            recv2[1, n] = grad

        return 0

    lax.fori_loop(1, MEMBER + 1, gradients_out, 0)
    for r in range(2):
        hidden_near(r, near_at).wait_recv()

        @pl.when(has_beyond)
        def _():
            hidden_far(r, near_at, far_at_beyond).start()

    pl.semaphore_wait(span4, 2)
    tell(span8, 8)

    def halo_prev(d, _):
        n = lax.rem(m + d, MEMBER)

        @pl.when(has_prev)
        def _():
            copy2(2, n, m, s - 1, n).start()

        return 0

    def halo_next(d, _):
        n = lax.rem(m + d, MEMBER)

        @pl.when(has_next)
        def _():
            copy2(0, n, m, s + 1, n).start()

        return 0

    lax.fori_loop(0, MEMBER, halo_next, 0)
    lax.fori_loop(0, MEMBER, halo_prev, 0)

    def wait_block(kind):
        def one(d, _):
            n = lax.rem(m + MEMBER - d, MEMBER)

            @pl.when(jnp.logical_or(kind != 1, d > 0))
            def _():
                copy2(kind, n, n, s, n).wait_recv()

            return 0

        lax.fori_loop(0, MEMBER, one, 0)

    def rows_ready(kind, half):
        q = 2 * kind + half
        ext[...] = jnp.zeros_like(ext)
        lane = lane_index(PK - CH)
        for k in range(8):
            chunk = recv2[kind, 8 * half + k].astype(F32)
            tail = chunk[CH:PK]
            low = jnp.where(lane < PX - 128, tail, 0.0)
            high = jnp.where(lane < PX - 128, pltpu.roll(tail, 64, 1), 0.0)
            rest = jnp.concatenate([low, high[0:32]], axis=0)
            wide = jnp.concatenate([chunk[0:CH], rest, jnp.zeros((CH, 128), F32)], axis=1)
            start = PX * k + 2
            base, off = start // 128 * 128, start % 128
            ext[:, base : base + 384] += pltpu.roll(wide, off, 1)
        first = ext[:, 0:128]
        last = ext[:, LP - 128 : LP]
        lane = lane_index(CH)
        ext[:, 0:128] = jnp.where(lane < 2, pltpu.roll(last, 96, 1), first)
        ext[:, LP - 128 : LP] = jnp.where(
            jnp.logical_and(lane >= 34, lane < 36), pltpu.roll(first, 32, 1), last
        )

        def piece(p):
            b, g = p // 9, p % 9
            if b == KW:
                return jnp.zeros((8, LP), F32)
            rows = ext[8 * g : 8 * g + 8, :]
            return pltpu.roll(rows, LP - b, 1) if b else rows

        for k in range(KP // 16):
            both = jnp.concatenate([piece(2 * k), piece(2 * k + 1)], axis=0)
            stack[q, 16 * k : 16 * k + 16, :] = both.astype(BF16)

    def block_rows(kind):
        def one(half, _):
            rows_ready(kind, half)
            return 0

        lax.fori_loop(0, 2, one, 0)

    def hidden_terms(kind):
        def one(half, _):
            q = 2 * kind + half
            out_acc[...] += jnp.dot(wst[q, :, 0:KP], stack[q], preferred_element_type=F32)
            return 0

        lax.fori_loop(0, 2, one, 0)

    wait_block(1)
    block_rows(1)

    from_beyond = s - 2 + 4 * side
    has_from = jnp.logical_and(from_beyond >= 0, from_beyond < SPACE)

    @pl.when(has_from)
    def _():
        for r in range(2):
            hidden_far(r, 0, 4 * side).wait_recv()

    def kernel_terms(half):
        rows = hid[half : half + KW].reshape(KW * CP, LP)
        return lax.dot_general(
            rows, stack[2 + half], (((1,), (1,)), ((), ())), preferred_element_type=F32
        )

    product = kernel_terms(0) + kernel_terms(1)
    total[...] = jnp.zeros_like(total)
    for t in range(KW):
        total[CH * t : CH * t + CH, 0:KP] = product[CP * t : CP * t + CH]

    def share_rows(u):
        return pl.ds(pl.multiple_of(SR * lax.rem(u, 9), 8), SR)

    def share_lanes(u):
        return pl.ds(pl.multiple_of(128 * (u // 9), 128), 128)

    def copy_a1(src, slot, space, member):
        return pltpu.make_async_remote_copy(
            src_ref=ar1_send.at[src],
            dst_ref=ar1_recv.at[slot],
            send_sem=a1_ssem.at[src],
            recv_sem=a1_rsem.at[slot],
            device_id={"space": space, "member": member},
        )

    def share_owner(u):
        return s - side + u // MEMBER, lax.rem(u, MEMBER)

    def shares_out(d, _):
        u = lax.rem(share_id + d, 2 * MEMBER)

        @pl.when(u < SHARES)
        def _():
            ar1_send[u] = total[share_rows(u), share_lanes(u)].astype(BF16)
            space, member = share_owner(u)
            copy_a1(u, share_id, space, member).start()

        return 0

    lax.fori_loop(1, 2 * MEMBER, shares_out, 0)

    hidden_terms(1)

    def z1(k, slot):
        return pltpu.make_async_remote_copy(
            src_ref=z1_send,
            dst_ref=z1_recv.at[slot],
            send_sem=z1_ssem.at[k],
            recv_sem=z1_rsem.at[slot],
            device_id={"space": block_mate(k), "member": m},
        )

    def z2(k, slot):
        return pltpu.make_async_remote_copy(
            src_ref=z2_send,
            dst_ref=z2_recv.at[slot],
            send_sem=z2_ssem.at[k],
            recv_sem=z2_rsem.at[slot],
            device_id={"space": comb_mate(k), "member": m},
        )

    def four(ref):
        a, b, c, d = (ref[k].astype(F32) for k in range(4))
        return (a + b) + (c + d)

    pl.semaphore_wait(span8, 2)

    @pl.when(holds_share)
    def _():
        def shares_in(d, acc):
            u = lax.rem(share_id + 2 * MEMBER - d, 2 * MEMBER)
            space, member = share_owner(u)
            copy_a1(0, u, space, member).wait_recv()
            return acc + ar1_recv[u].astype(F32)

        own = total[share_rows(share_id), share_lanes(share_id)]
        acc = lax.fori_loop(1, 2 * MEMBER, shares_in, own).astype(BF16)
        z1_send[...] = acc
        z1_recv[z_low] = acc
        for k in (1, 2, 3):
            z1(k, z_low).start()

    @pl.when(has_prev)
    def _():
        wait_block(0)
        block_rows(0)
        hidden_terms(0)

    @pl.when(holds_share)
    def _():
        for k in (1, 2, 3):
            z1(k, lax.rem(z_low + k, 4)).wait_recv()
        acc = four(z1_recv).astype(BF16)
        z2_send[...] = acc
        z2_recv[z_high] = acc
        for k in (1, 2, 3):
            z2(k, z_high).start()

    @pl.when(has_next)
    def _():
        wait_block(2)
        block_rows(2)
        hidden_terms(2)

    norm = float(1.0 / np.sqrt(np.float32(MEMBER * 2 * SPACE * LON)))

    def copy_a4(u, slot, space, member):
        return pltpu.make_async_remote_copy(
            src_ref=ar4_send,
            dst_ref=ar4_recv.at[slot],
            send_sem=a4_ssem.at[u],
            recv_sem=a4_rsem.at[slot],
            device_id={"space": space, "member": member},
        )

    @pl.when(holds_share)
    def _():
        for k in (1, 2, 3):
            z2(k, lax.rem(z_high + k, 4)).wait_recv()
        final = (four(z2_recv) * norm).astype(BF16)
        ar4_send[...] = final
        total[share_rows(share_id), share_lanes(share_id)] = final.astype(F32)

        def totals_out(d, _):
            u = lax.rem(share_id + d, 2 * MEMBER)
            space, member = share_owner(u)
            copy_a4(u, share_id, space, member).start()
            return 0

        lax.fori_loop(1, 2 * MEMBER, totals_out, 0)

    back_ref[0] = out_acc[0:CH, 0:LON].astype(BF16)
    back_ref[1] = out_acc[CP : CP + CH, 0:LON].astype(BF16)

    def totals_in(d, _):
        u = lax.rem(share_id + 2 * MEMBER - d, 2 * MEMBER)

        @pl.when(u < SHARES)
        def _():
            space, member = share_owner(u)
            copy_a4(0, u, space, member).wait_recv()
            total[share_rows(u), share_lanes(u)] = ar4_recv[u].astype(F32)

        return 0

    lax.fori_loop(1, 2 * MEMBER, totals_in, 0)
    for a in range(KW):
        for b in range(KW):
            base, off = CH * b // 128 * 128, CH * b % 128
            width = 256 if off + CH > 128 else 128
            part = total[CH * (4 - a) : CH * (5 - a), base : base + width]
            if off:
                part = pltpu.roll(part, width - off, 1)
            kgrad_ref[KW * a + b] = part[:, 0:CH]

    def sent(d, _):
        n = lax.rem(m + d, MEMBER)
        copy1(n, m, n).wait_send()
        copy2(1, n, m, s, n).wait_send()
        return 0

    lax.fori_loop(1, MEMBER, sent, 0)

    def halo_sent(d, _):
        n = lax.rem(m + d, MEMBER)

        @pl.when(has_prev)
        def _():
            copy2(2, n, m, s - 1, n).wait_send()

        @pl.when(has_next)
        def _():
            copy2(0, n, m, s + 1, n).wait_send()

        return 0

    lax.fori_loop(0, MEMBER, halo_sent, 0)

    def shares_sent(d, _):
        u = lax.rem(share_id + d, 2 * MEMBER)
        space, member = share_owner(u)

        @pl.when(u < SHARES)
        def _():
            copy_a1(u, share_id, space, member).wait_send()

        @pl.when(holds_share)
        def _():
            copy_a4(u, share_id, space, member).wait_send()

        return 0

    lax.fori_loop(1, 2 * MEMBER, shares_sent, 0)
    for r in range(2):
        hidden_near(r, far_at).wait_send()

        @pl.when(has_beyond)
        def _():
            hidden_far(r, near_at, far_at_beyond).wait_send()

    @pl.when(holds_share)
    def _():
        for k in (1, 2, 3):
            z1(k, z_low).wait_send()
            z2(k, z_high).wait_send()


def call(weights, pred, truth, scale, hidden, filters):
    vmem = pl.BlockSpec(memory_space=pltpu.VMEM)
    dma = pltpu.SemaphoreType.DMA
    return pl.pallas_call(
        kernel,
        out_shape=(
            jax.ShapeDtypeStruct((2, CH, LON), BF16),
            jax.ShapeDtypeStruct((KW * KW, CH, CH), F32),
        ),
        in_specs=[pl.BlockSpec(memory_space=pltpu.SMEM)] + [vmem] * 5,
        out_specs=(vmem, vmem),
        scratch_shapes=[
            pltpu.VMEM((MEMBER, PK, 128), BF16),
            pltpu.VMEM((MEMBER, PK, 128), BF16),
            pltpu.VMEM((2 * MEMBER * PK, 128), F32),
            pltpu.VMEM((PK, 128), F32),
            pltpu.VMEM((PK, 128), F32),
            pltpu.VMEM((MEMBER * PK, 128), F32),
            pltpu.VMEM((CH, 256), F32),
            pltpu.VMEM((CP, 128), F32),
            pltpu.VMEM((MEMBER, PK, 128), BF16),
            pltpu.VMEM((3, MEMBER, PK, 128), BF16),
            pltpu.VMEM((6, CP, LP), BF16),
            pltpu.VMEM((CH, LP), F32),
            pltpu.VMEM((6, KP, LP), BF16),
            pltpu.VMEM((6, 2 * CP, 384), BF16),
            pltpu.VMEM((KC, 384), F32),
            pltpu.VMEM((2 * CP, LP), F32),
            pltpu.VMEM((2 * MEMBER, SR, 128), BF16),
            pltpu.VMEM((2 * MEMBER, SR, 128), BF16),
            pltpu.VMEM((SR, 128), BF16),
            pltpu.VMEM((4, SR, 128), BF16),
            pltpu.VMEM((SR, 128), BF16),
            pltpu.VMEM((4, SR, 128), BF16),
            pltpu.VMEM((SR, 128), BF16),
            pltpu.VMEM((2 * MEMBER, SR, 128), BF16),
            dma((MEMBER,)),
            dma((MEMBER,)),
            dma((2,)),
            dma((2,)),
            dma((2,)),
            dma((2,)),
            dma((3, MEMBER)),
            dma((3, MEMBER)),
            dma((2 * MEMBER,)),
            dma((2 * MEMBER,)),
            dma((4,)),
            dma((4,)),
            dma((4,)),
            dma((4,)),
            dma((2 * MEMBER,)),
            dma((2 * MEMBER,)),
            pltpu.SemaphoreType.REGULAR,
            pltpu.SemaphoreType.REGULAR,
            pltpu.SemaphoreType.REGULAR,
            pltpu.SemaphoreType.REGULAR,
        ],
        compiler_params=pltpu.CompilerParams(
            collective_id=0, has_side_effects=True, vmem_limit_bytes=48 * 1024 * 1024
        ),
    )(weights, pred, truth, scale, hidden, filters)


def body(prediction_maps, truth_analysis, reciprocal_spread, deconv_inputs, filter_tensor):
    rows = 2 * SPACE
    index = np.arange(rows, dtype=np.float64)
    cosine = np.cos((index + 0.5) * (np.pi / rows) - np.pi / 2)
    weights = jnp.asarray((cosine / cosine.mean()).astype(np.float32))
    pred = jnp.pad(jnp.transpose(prediction_maps[0], (1, 0, 2)), ((0, 0), (0, 0), (0, LP - LON)))
    hidden = jnp.pad(
        jnp.transpose(deconv_inputs[0], (1, 0, 2)), ((0, 0), (0, CP - CH), (0, LP - LON))
    )
    back, kgrad = call(
        weights, pred, truth_analysis, reciprocal_spread.reshape(1, CH), hidden, filter_tensor
    )
    return jnp.transpose(back, (1, 0, 2))[None], kgrad.reshape(KW, KW, CH, CH)


def solution(mesh):
    return jax.shard_map(
        body,
        mesh=mesh,
        in_specs=(
            P("member", None, "space", None),
            P(None, ("space", "member")),
            P(),
            P("member", None, "space", None),
            P(),
        ),
        out_specs=(P("member", None, "space", None), P()),
        check_vma=False,
    )
```
